256 devices in a mesh: frame: 16 (over y_lo, z), row: 16 (over y_hi, x, core).
Axes of the slice: x: 4, y: 4 (y_hi: 2, y_lo: 2; y = y_hi * 2 + y_lo), z: 8, core: 2. Of those that a mesh axis runs over, the one named last changes fastest.
Arguments:
- clip_tokens: bfloat16 [64, 32, 40, 1152], P('frame', 'row'), may hold values from -6 to 6
- modulation: float32 [6, 1152], replicated, may hold values from -3 to 3
- w_sqkv: bfloat16 [1152, 3456], P(None, 'frame'), may hold values from -1.5 to 1.5
- w_sout: bfloat16 [1152, 1152], P(None, 'frame'), may hold values from -0.1875 to 0.1875
- w_tqkv: bfloat16 [1152, 3456], P(None, 'frame'), may hold values from -1.5 to 1.5
- w_tout: bfloat16 [1152, 1152], P(None, 'frame'), may hold values from -0.1875 to 0.1875
Outputs:
- block_out: bfloat16 [64, 32, 40, 1152], P('frame', 'row')
The draws below stay inside these ranges and needn't reach their ends.
All inputs are finite; a program needn't handle non-finite values.
Results may differ from the reference program's by a relative error of at most 0.009.
Values may be sent and summed in bfloat16 or wider, within the bound.
No kernel may reach another device: no remote copies, remote signals or barrier semaphores. Data moves between devices by JAX's collectives and lax.ppermute only.
A program may use at most 128 MiB of HBM per device.

```python
import math
import jax
import jax.numpy as jnp
from jax import lax

D = 1152
HEADS = 16
HEAD_DIM = 72
PW = 40
FRAMES = 64
ROWS = 32


def drawn_projection(key, low_end, high_end):
    key_base, key_noise, key_value, key_scale = jax.random.split(key, 4)
    base_part = jax.random.truncated_normal(key_base, -6.0, 6.0, (D, D), jnp.float32) * D ** (-0.5)
    noise_part = jax.random.truncated_normal(key_noise, -6.0, 6.0, (D, D), jnp.float32) * D ** (-0.5)
    value_part = jax.random.truncated_normal(key_value, -6.0, 6.0, (D, D), jnp.float32) * D ** (-0.5)
    head_scale = jnp.exp(jax.random.uniform(key_scale, (HEADS, 1), jnp.float32, math.log(low_end), math.log(high_end)))
    head_scale = jnp.broadcast_to(head_scale, (HEADS, HEAD_DIM)).reshape(1, D)
    query_part = base_part * head_scale
    key_part = noise_part * head_scale
    return jnp.clip(jnp.concatenate([query_part, key_part, value_part], axis=1), -1.5, 1.5)


def draw_w_sqkv(key, part):
    key = jax.random.fold_in(key, 11)
    return drawn_projection(key, 1.0, 1.0).astype(jnp.bfloat16)


def draw_w_tqkv(key, part):
    key = jax.random.fold_in(key, 23)
    return drawn_projection(key, 1.0, 1.0).astype(jnp.bfloat16)


def block_scale(key, shape, shards, smallest, high):
    def one(axis_at, shards_of):
        draws = jax.random.uniform(jax.random.fold_in(jax.random.fold_in(key, 6), axis_at), (shards_of,), jnp.float32, smallest / len(shards), high / len(shards))
        return jnp.repeat(jnp.exp(draws), shape[axis_at] // shards_of).reshape((-1,) + (1,) * (len(shape) - axis_at - 1))

    factor_of = one(*shards[0])
    for cut in shards[1:]:
        factor_of = factor_of * one(*cut)
    return factor_of


def gaussian(own_key, extent, width, reach, pieces=(), kind=jnp.bfloat16):
    array = jax.random.normal(own_key, extent, jnp.float32) * width
    if len(pieces) > 0:
        array = block_scale(own_key, extent, pieces, -0.22, 0.18) * array
    return jnp.clip(array, min=-reach, max=reach).astype(kind)


def setup_inputs(seed: int = 0) -> dict:
    keys = jax.random.split(jax.random.key(seed), 7)
    return {
        "clip_tokens": gaussian(keys[0], (FRAMES, ROWS, PW, D), 1.0, 6.0, ((0, 16), (1, 16))),
        "modulation": gaussian(keys[1], (6, D), 0.7, 3.0, (), jnp.float32),
        "w_sqkv": draw_w_sqkv(jax.random.fold_in(keys[6], 71), 0),
        "w_sout": gaussian(keys[3], (D, D), D ** -0.5, 0.1875, ((1, 16),)),
        "w_tqkv": draw_w_tqkv(jax.random.fold_in(keys[6], 71), 0),
        "w_tout": gaussian(keys[5], (D, D), D ** -0.5, 0.1875, ((1, 16),)),
    }


def layer_norm(inputs):
    average = lax.optimization_barrier(jnp.mean(inputs, axis=-1, keepdims=True))
    centered = inputs - average
    variance = lax.optimization_barrier(jnp.mean(centered * centered, axis=-1, keepdims=True))
    return centered * lax.rsqrt(variance + 1e-06)

def modulate(inputs, shift, scale):
    return (layer_norm(inputs) * (1.0 + scale) + shift).astype(jnp.bfloat16)

def frame_attention(qkv_block):
    queries = qkv_block[:, 0].astype(jnp.float32)
    key_rows = qkv_block[:, 1].astype(jnp.float32)
    values = qkv_block[:, 2].astype(jnp.float32)
    scores = jnp.einsum('qhd,khd->hqk', queries, key_rows) / jnp.sqrt(jnp.float32(HEAD_DIM))
    peak_score = lax.optimization_barrier(jnp.max(scores, axis=-1, keepdims=True))
    exp_scores = jnp.exp(scores - peak_score)
    weights = (exp_scores / lax.optimization_barrier(jnp.sum(exp_scores, axis=-1, keepdims=True))).astype(jnp.bfloat16)
    return jnp.einsum('hqk,khd->qhd', weights.astype(jnp.float32), values).astype(jnp.bfloat16)

def head_temporal(qkv_block):
    queries = qkv_block[:, :, 0].astype(jnp.float32)
    key_rows = qkv_block[:, :, 1].astype(jnp.float32)
    values = qkv_block[:, :, 2].astype(jnp.float32)
    scores = jnp.einsum('fpd,gpd->pfg', queries, key_rows) / jnp.sqrt(jnp.float32(HEAD_DIM))
    peak_score = lax.optimization_barrier(jnp.max(scores, axis=-1, keepdims=True))
    exp_scores = jnp.exp(scores - peak_score)
    weights = (exp_scores / lax.optimization_barrier(jnp.sum(exp_scores, axis=-1, keepdims=True))).astype(jnp.bfloat16)
    return jnp.einsum('pfg,gpd->fpd', weights.astype(jnp.float32), values).astype(jnp.bfloat16)

def reference(clip_tokens, modulation, w_sqkv, w_sout, w_tqkv, w_tout):
    tok_count = ROWS * PW
    clip_float = clip_tokens.astype(jnp.float32).reshape(FRAMES, tok_count, D)
    normed = modulate(clip_float, modulation[0], modulation[1])
    qkv_s = jnp.dot(normed.reshape(-1, D), w_sqkv, preferred_element_type=jnp.float32).astype(jnp.bfloat16)
    qkv_s = qkv_s.reshape(FRAMES, tok_count, 3, HEADS, HEAD_DIM)
    out_s = lax.map(frame_attention, qkv_s).reshape(-1, D)
    residual_mid = clip_float + modulation[2] * jnp.dot(out_s, w_sout, preferred_element_type=jnp.float32).reshape(FRAMES, tok_count, D)
    normed_t = modulate(residual_mid, modulation[3], modulation[4])
    qkv_t = jnp.dot(normed_t.reshape(-1, D), w_tqkv, preferred_element_type=jnp.float32).astype(jnp.bfloat16)
    qkv_t = jnp.moveaxis(qkv_t.reshape(FRAMES, tok_count, 3, HEADS, HEAD_DIM), 3, 0)
    out_t = jnp.moveaxis(lax.map(head_temporal, qkv_t), 0, 2).reshape(-1, D)
    block_out = residual_mid + modulation[5] * jnp.dot(out_t, w_tout, preferred_element_type=jnp.float32).reshape(FRAMES, tok_count, D)
    return block_out.astype(jnp.bfloat16).reshape(FRAMES, ROWS, PW, D)
```

```python
import functools
import math

import jax
import jax.numpy as jnp
from jax import lax
from jax.experimental import pallas as pl
from jax.experimental.pallas import tpu as pltpu
from jax.sharding import PartitionSpec as P

HEADS = 16
HEAD_DIM = 72
D = 1152
GROUP = 4 * HEAD_DIM
PAD = 80
BF = jnp.bfloat16
F32 = jnp.float32
SCALE = math.log2(math.e) / math.sqrt(HEAD_DIM)
VMEM = pl.BlockSpec(memory_space=pltpu.VMEM)
ANY = pl.BlockSpec(memory_space=pl.ANY)
NT = (((1,), (1,)), ((), ()))


def params(mib):
    return pltpu.CompilerParams(vmem_limit_bytes=mib * 1024 * 1024)


def normalize(inputs, shift, scale):
    average = jnp.mean(inputs, axis=-1, keepdims=True)
    centered = inputs - average
    variance = jnp.mean(centered * centered, axis=-1, keepdims=True)
    return (centered * lax.rsqrt(variance + 1e-06) * (1.0 + scale) + shift).astype(BF)


def place():
    r = lax.axis_index("row")
    return r >> 3, (r >> 1) & 3, r & 1


def repack_kernel(w_ref, out_ref):
    _, x, _ = place()
    for g in range(4):

        @pl.when(x == g)
        def _(g=g):
            cols = []
            for part in range(3):
                for h in range(4):
                    p = 16 * part + 4 * g + h
                    cols.append(w_ref[p // 3, :, 72 * (p % 3) : 72 * (p % 3) + 72])
            out_ref[...] = jnp.concatenate(cols, axis=1)


def join_kernel(w_ref, out_ref):
    out_ref[...] = jnp.concatenate([w_ref[i] for i in range(16)], axis=0)


def gate_kernel(*refs):
    refs[-1][...] = jnp.zeros_like(refs[-1])


def spatial_kernel(a, b, c_, d_, w0, w1, o_ref, w_scr, q_scr, k_scr, v_scr):
    yh, x, c = place()
    for s, w in enumerate((w0, w1)):
        w_scr[pl.ds(pl.multiple_of(576 * (c ^ s), 64), 576), :] = w[...]
    lane = lax.broadcasted_iota(jnp.int32, (320, 128 - HEAD_DIM), 1)
    zeros = jnp.zeros((320, 128 - HEAD_DIM), BF)
    ones = jnp.where(lane == 0, 1.0, 0.0).astype(BF)
    for i, ref in enumerate((a, b, c_, d_)):
        rows = slice(320 * i, 320 * i + 320)
        qkv = jnp.dot(ref[...], w_scr[...], preferred_element_type=F32)
        for h in range(4):
            lo = 72 * h
            q = (qkv[:, lo : lo + 72] * SCALE).astype(BF)
            k = qkv[:, GROUP + lo : GROUP + lo + 72].astype(BF)
            v = qkv[:, 2 * GROUP + lo : 2 * GROUP + lo + 72].astype(BF)
            q_scr[h, rows, :] = jnp.concatenate([q, zeros], axis=1)
            k_scr[h, rows, :] = jnp.concatenate([k, zeros], axis=1)
            v_scr[h, rows, :] = jnp.concatenate([v, ones], axis=1)

    def step(i, carry):
        heads = []
        for h in range(4):
            q = q_scr[h, pl.ds(pl.multiple_of(320 * i, 64), 320), :]
            s = lax.dot_general(q, k_scr[h], NT, preferred_element_type=F32)
            m = jnp.max(s, axis=-1, keepdims=True)
            p = jnp.exp2(s - m).astype(BF)
            o = jnp.dot(p, v_scr[h], preferred_element_type=F32)
            heads.append((o[:, :72] / o[:, 72:73]).astype(BF))
        out = jnp.concatenate(heads, axis=1)
        for t in range(4):
            dest = (yh ^ (t & 1)) * 8 + ((x - i) & 3) * 2 + (c ^ (t >> 1))
            o_ref[dest] = out[80 * t : 80 * t + 80]
        return carry

    lax.fori_loop(0, 4, step, 0)


def spread(frame_major):
    if frame_major:
        row = lax.broadcasted_iota(jnp.int32, (512, 320), 0)
        col = lax.broadcasted_iota(jnp.int32, (512, 320), 1)
    else:
        row = lax.broadcasted_iota(jnp.int32, (320, 512), 1)
        col = lax.broadcasted_iota(jnp.int32, (320, 512), 0)
    f, t = row >> 5, row & 31
    j = (t * 13) >> 6
    want = 80 * j + 5 * f + (t - 5 * j)
    return jnp.where((t < 20) & (col == want), 1.0, 0.0).astype(BF)


def compact(narrow):
    if narrow:
        wide = lax.broadcasted_iota(jnp.int32, (320, 512), 1)
        thin = lax.broadcasted_iota(jnp.int32, (320, 512), 0)
    else:
        wide = lax.broadcasted_iota(jnp.int32, (512, 320), 0)
        thin = lax.broadcasted_iota(jnp.int32, (512, 320), 1)
    f, t = wide >> 5, wide & 31
    return jnp.where((t < 20) & (thin == 20 * f + t), 1.0, 0.0).astype(BF)


def unpack_chunks(ref, scr):
    zeros = jnp.zeros((12, D), BF)
    for f in range(16):
        scr[32 * f : 32 * f + 32, :] = jnp.concatenate([ref[f], zeros], axis=0)
    return scr[...]


def both_halves(x, mine_ref, other_ref):
    c = lax.axis_index("row") & 1
    mine = lax.dot_general(x, mine_ref[...], NT, preferred_element_type=F32)
    other = lax.dot_general(x, other_ref[...], NT, preferred_element_type=F32)
    return jnp.where(c == 0, mine, other), jnp.where(c == 0, other, mine)


def middle_kernel(o_ref, clip_ref, mod_ref, mine_ref, other_ref, mid_ref, out_ref):
    groups = [
        jnp.concatenate([o_ref[8 * (j >> 1) + 2 * g + (j & 1)] for j in range(4)], axis=0) for g in range(4)
    ]
    total = jnp.concatenate(both_halves(jnp.concatenate(groups, axis=1), mine_ref, other_ref), axis=1)
    mid = clip_ref[...].astype(F32) + mod_ref[2:3, :] * total
    mid_ref[...] = mid
    normed = normalize(mid, mod_ref[3:4, :], mod_ref[4:5, :])
    out = jnp.dot(spread(True), normed, preferred_element_type=F32).astype(BF)
    for f in range(16):
        out_ref[f] = out[32 * f : 32 * f + 20]


def temporal_kernel(x_ref, mine_ref, other_ref, o_ref, scr):
    x = jnp.dot(compact(True), unpack_chunks(x_ref, scr), preferred_element_type=F32).astype(BF)
    halves = both_halves(x, mine_ref, other_ref)

    def part(p):
        lo = PAD * (p % 24)
        return halves[p // 24][:, lo : lo + PAD]

    row = lax.broadcasted_iota(jnp.int32, (320, 320), 0)
    col = lax.broadcasted_iota(jnp.int32, (320, 320), 1)
    same = lax.rem(row, 5) == lax.rem(col, 5)
    heads = []
    for h in range(HEADS):
        q = (part(h) * SCALE).astype(BF)
        k = part(16 + h).astype(BF)
        v = part(32 + h).astype(BF)
        s = lax.dot_general(q, k, NT, preferred_element_type=F32)
        s = jnp.where(same, s, -1e30)
        m = jnp.max(s, axis=-1, keepdims=True)
        p = jnp.exp2(s - m)
        total = jnp.sum(p, axis=-1, keepdims=True)
        o = jnp.dot(p.astype(BF), v, preferred_element_type=F32) / total
        heads.append(o[:, :72].astype(BF))
    o = jnp.concatenate(heads, axis=1)
    out = jnp.dot(compact(False), o, preferred_element_type=F32).astype(BF)
    for f in range(16):
        o_ref[f] = out[32 * f : 32 * f + 20]


def final_kernel(o_ref, mid_ref, mod_ref, mine_ref, other_ref, out_ref, scr):
    o = jnp.dot(spread(False), unpack_chunks(o_ref, scr), preferred_element_type=F32).astype(BF)
    y = jnp.concatenate(both_halves(o, mine_ref, other_ref), axis=1)
    out_ref[...] = (mid_ref[...] + mod_ref[5:6, :] * y).astype(BF)


def shift_x(value, d):
    pairs = [(r, (r & 9) | ((((r >> 1) + d) & 3) << 1)) for r in range(16)]
    return lax.ppermute(value, "row", pairs)


def swap_core(value):
    return lax.ppermute(value, "row", [(r, r ^ 1) for r in range(16)])


def swap_yh(value):
    return lax.ppermute(value, "row", [(r, r ^ 8) for r in range(16)])


def take_half(value):
    y_lo = lax.axis_index("frame") >> 3
    pairs = [
        (16 * f + r, 16 * (f ^ 8) + r) for f in range(16) for r in range(16) if f >> 3 != r & 1
    ]
    pairs = [(src, dst) for dst, src in pairs]
    moved = lax.ppermute(value, ("frame", "row"), pairs)
    c = lax.axis_index("row") & 1
    return jnp.where(c == y_lo, value, moved)


def gather_half(value):
    rings = [list(range(8)), list(range(8, 16))]
    return lax.all_gather(value, "frame", axis=0, tiled=True, axis_index_groups=rings)


def call(kernel, outs, n_in, scratch=(), mib=40, any_in=(), us=2):
    return pl.pallas_call(
        kernel,
        out_shape=outs,
        in_specs=[ANY if i in any_in else VMEM for i in range(n_in)],
        out_specs=jax.tree.map(lambda _: VMEM, outs),
        scratch_shapes=list(scratch),
        compiler_params=params(mib),
        cost_estimate=pl.CostEstimate(flops=us * 10**9, bytes_accessed=us * 10**6, transcendentals=0),
    )


def sds(shape, dtype=BF):
    return jax.ShapeDtypeStruct(shape, dtype)


def on_device(clip_tokens, modulation, w_sqkv, w_sout, w_tqkv, w_tout):
    frames_here, rows_here, patches, features = clip_tokens.shape
    tokens = rows_here * patches
    yh, x, c = place()

    clip = clip_tokens.reshape(frames_here, tokens, features)
    normed = normalize(clip.astype(F32), modulation[0], modulation[1])
    first = lax.dynamic_slice(w_sqkv, (576 * c, 0), (576, 216))
    normed, first, w_sout, w_tout = lax.optimization_barrier((normed, first, w_sout, w_tout))

    own = lax.dynamic_slice_in_dim(normed, 2 * yh, 2, 0)
    theirs = swap_yh(lax.dynamic_slice_in_dim(normed, 2 * (1 - yh), 2, 0))
    outs = gather_half(take_half(jnp.concatenate([w_sout.T, w_tout.T], axis=0)))
    first = lax.all_to_all(first.reshape(16, 36, 216), "frame", 0, 0, tiled=True)
    first, w_tqkv = lax.optimization_barrier((first, w_tqkv))
    second = call(repack_kernel, sds((36, 3 * GROUP)), 1)(first)
    give = jnp.stack([own[1 - c], theirs[1 - c]])
    keep = jnp.stack([own[c], theirs[c]])
    g1 = jnp.concatenate([keep, swap_core(give)], axis=0).reshape(320, D)
    g = [g1] + [shift_x(g1, d) for d in (1, 2, 3)]
    gate = call(gate_kernel, sds((8, 128), F32), 4, any_in=(0, 1, 2, 3), us=2000)(*g)
    second = lax.all_to_all(jnp.broadcast_to(second[None], (16, 36, 3 * GROUP)), "frame", 0, 0, tiled=True)
    tq = jnp.pad(w_tqkv.T.reshape(3, 72, D), ((0, 0), (0, 8), (0, 0))).reshape(3 * PAD, D)
    *g, second, tq, _ = lax.optimization_barrier((*g, second, take_half(tq), gate))
    w_mine = call(join_kernel, sds((576, 3 * GROUP)), 1)(second)
    w_other = swap_core(w_mine)
    t_mine = gather_half(tq)

    o_s = call(
        spatial_kernel,
        sds((16, tokens, GROUP)),
        6,
        scratch=[
            pltpu.VMEM((D, 3 * GROUP), BF),
            pltpu.VMEM((4, 1280, 128), BF),
            pltpu.VMEM((4, 1280, 128), BF),
            pltpu.VMEM((4, 1280, 128), BF),
        ],
        us=15,
    )(*g, w_mine, w_other)
    o_s, outs = lax.optimization_barrier((o_s, outs))
    outs_other = swap_core(outs)
    outs = outs.reshape(8, 2, 72, D)
    outs_other = outs_other.reshape(8, 2, 72, D)
    out_s = [v[:, 0].reshape(576, D) for v in (outs, outs_other)]
    out_t = [v[:, 1].reshape(576, D) for v in (outs, outs_other)]
    o_s = lax.all_to_all(o_s, "row", 0, 0, tiled=True)

    mid, chunks = call(middle_kernel, (sds((320, D), F32), sds((16, 20, D))), 5, us=4)(
        o_s, clip.reshape(320, D), modulation, *out_s
    )
    chunks, t_mine = lax.optimization_barrier((chunks, t_mine))
    t_other = swap_core(t_mine)
    chunks = lax.all_to_all(chunks, "frame", 0, 0, tiled=True)
    o_t = call(temporal_kernel, sds((16, 20, D)), 3, scratch=[pltpu.VMEM((512, D), BF)], us=12)(
        chunks, t_mine, t_other
    )
    o_t = lax.all_to_all(o_t, "frame", 0, 0, tiled=True)
    out = call(final_kernel, sds((320, D)), 5, scratch=[pltpu.VMEM((512, D), BF)], us=4)(
        o_t, mid, modulation, *out_t
    )
    return out.reshape(frames_here, rows_here, patches, features)


def solution(mesh):
    in_specs = (
        P("frame", "row", None, None),
        P(),
        P(None, "frame"),
        P(None, "frame"),
        P(None, "frame"),
        P(None, "frame"),
    )
    out_specs = P("frame", "row", None, None)
    return jax.shard_map(
        on_device, mesh=mesh, in_specs=in_specs, out_specs=out_specs, check_vma=False
    )
```

```python
import functools
import math

import jax
import jax.numpy as jnp
from jax import lax
from jax.experimental import pallas as pl
from jax.experimental.pallas import tpu as pltpu
from jax.sharding import PartitionSpec as P

HEADS = 16
HEAD_DIM = 72
D = 1152
GROUP = 4 * HEAD_DIM
PAD = 80
BF = jnp.bfloat16
F32 = jnp.float32
SCALE = math.log2(math.e) / math.sqrt(HEAD_DIM)
VMEM = pl.BlockSpec(memory_space=pltpu.VMEM)
ANY = pl.BlockSpec(memory_space=pl.ANY)
NT = (((1,), (1,)), ((), ()))


def params(mib):
    return pltpu.CompilerParams(vmem_limit_bytes=mib * 1024 * 1024)


def normalize(inputs, shift, scale):
    average = jnp.mean(inputs, axis=-1, keepdims=True)
    centered = inputs - average
    variance = jnp.mean(centered * centered, axis=-1, keepdims=True)
    return (centered * lax.rsqrt(variance + 1e-06) * (1.0 + scale) + shift).astype(BF)


def place():
    r = lax.axis_index("row")
    return r >> 3, (r >> 1) & 3, r & 1


def norm_kernel(clip_ref, mod_ref, keep_ref, swap_ref, give_ref):
    yh, _, c = place()

    def normed(j):
        return normalize(clip_ref[j].astype(F32), mod_ref[0:1, :], mod_ref[1:2, :])

    keep_ref[...] = normed(2 * yh + c)
    swap_ref[...] = normed(2 * yh + 1 - c)
    for i in range(2):
        give_ref[i] = normed(2 * (1 - yh) + i)


def prepare_kernel(qkv_ref, sout_ref, tout_ref, proj_ref, out_ref):
    c = lax.axis_index("row") & 1
    for core, (lo, mid, width, proj) in enumerate(((0, 144, 40, sout_ref), (72, 184, 32, tout_ref))):

        @pl.when(c == core)
        def _(lo=lo, mid=mid, width=width, proj=proj):
            w = qkv_ref[...].astype(F32)
            rows = [w[lo : lo + 72], jnp.zeros((8, D), F32), w[mid : mid + width], jnp.zeros((48 - width, D), F32)]
            out_ref[...] = jnp.concatenate(rows, axis=0).astype(BF)
            proj_ref[...] = proj[...]


def repack_kernel(w_ref, out_ref):
    _, x, _ = place()
    for g in range(4):

        @pl.when(x == g)
        def _(g=g):
            cols = []
            for part in range(3):
                for h in range(4):
                    p = 16 * part + 4 * g + h
                    cols.append(w_ref[p // 3, :, 72 * (p % 3) : 72 * (p % 3) + 72])
            block = jnp.concatenate(cols, axis=1)
            block = jnp.concatenate([block, jnp.zeros((4, 3 * GROUP), BF)], axis=0)
            for f in range(16):
                out_ref[f] = block


def launch(pairs, sems):
    copies = [pltpu.make_async_copy(src, dst, sems.at[i]) for i, (src, dst) in enumerate(pairs)]
    for copy in copies:
        copy.start()
    return copies


def spatial_kernel(*refs):
    tokens, (w0, w1, o_ref, x_scr, w_in, w_scr, q_scr, k_scr, v_scr, out_scr, in_sems, out_sems) = refs[:8], refs[8:]
    yh, x, c = place()
    pairs = [(w, w_in.at[s]) for s, w in enumerate((w0, w1))]
    pairs += [(ref, x_scr.at[pl.ds(160 * i, 160)]) for i, ref in enumerate(tokens)]
    weights, copies = (lambda started: (started[:2], started[2:]))(launch(pairs, in_sems))
    for s, copy in enumerate(weights):
        copy.wait()
        rows = pl.ds(pl.multiple_of(576 * (c ^ s), 64), 576)
        w_scr[rows, :] = jnp.concatenate([w_in[s, i, :36] for i in range(16)], axis=0)
    lane = lax.broadcasted_iota(jnp.int32, (320, 128 - HEAD_DIM), 1)
    zeros = jnp.zeros((320, 128 - HEAD_DIM), BF)
    ones = jnp.where(lane == 0, 1.0, 0.0).astype(BF)
    for i in range(4):
        for copy in copies[2 * i : 2 * i + 2]:
            copy.wait()
        rows = slice(320 * i, 320 * i + 320)
        qkv = jnp.dot(x_scr[rows, :], w_scr[...], preferred_element_type=F32)
        for h in range(4):
            lo = 72 * h
            q = (qkv[:, lo : lo + 72] * SCALE).astype(BF)
            k = qkv[:, GROUP + lo : GROUP + lo + 72].astype(BF)
            v = qkv[:, 2 * GROUP + lo : 2 * GROUP + lo + 72].astype(BF)
            q_scr[h, rows, :] = jnp.concatenate([q, zeros], axis=1)
            k_scr[h, rows, :] = jnp.concatenate([k, zeros], axis=1)
            v_scr[h, rows, :] = jnp.concatenate([v, ones], axis=1)

    def outgoing(i, t):
        dest = (yh ^ (t >> 1)) * 8 + ((x - i) & 3) * 2 + (c ^ (t & 1))
        return pltpu.make_async_copy(out_scr.at[i, pl.ds(80 * t, 80)], o_ref.at[dest], out_sems.at[i, t])

    for i in range(4):
        heads = []
        for h in range(4):
            q = q_scr[h, 320 * i : 320 * i + 320, :]
            s = lax.dot_general(q, k_scr[h], NT, preferred_element_type=F32)
            m = jnp.max(s, axis=-1, keepdims=True)
            p = jnp.exp2(s - m).astype(BF)
            o = jnp.dot(p, v_scr[h], preferred_element_type=F32)
            heads.append((o[:, :72] / o[:, 72:73]).astype(BF))
        out_scr[i] = jnp.concatenate(heads, axis=1)
        for t in range(4):
            outgoing(i, t).start()
    for i in range(4):
        for t in range(4):
            outgoing(i, t).wait()


def spread(frame_major):
    if frame_major:
        row = lax.broadcasted_iota(jnp.int32, (512, 320), 0)
        col = lax.broadcasted_iota(jnp.int32, (512, 320), 1)
    else:
        row = lax.broadcasted_iota(jnp.int32, (320, 512), 1)
        col = lax.broadcasted_iota(jnp.int32, (320, 512), 0)
    f, t = row >> 5, row & 31
    j = (t * 13) >> 6
    want = 80 * j + 5 * f + (t - 5 * j)
    return jnp.where((t < 20) & (col == want), 1.0, 0.0).astype(BF)


def compact(narrow):
    if narrow:
        wide = lax.broadcasted_iota(jnp.int32, (320, 512), 1)
        thin = lax.broadcasted_iota(jnp.int32, (320, 512), 0)
    else:
        wide = lax.broadcasted_iota(jnp.int32, (512, 320), 0)
        thin = lax.broadcasted_iota(jnp.int32, (512, 320), 1)
    f, t = wide >> 5, wide & 31
    j = (t * 13) >> 6
    return jnp.where((t < 20) & (thin == 64 * (t - 5 * j) + 4 * f + j), 1.0, 0.0).astype(BF)


def unpack_chunks(ref, scr):
    zeros = jnp.zeros((8, D), BF)
    for f in range(16):
        scr[32 * f : 32 * f + 32, :] = jnp.concatenate([ref[f], zeros], axis=0)
    return scr[...]


def fetch_projection(core, mine, other, w_scr, sems):
    c = lax.axis_index("row") & 1
    y_lo = lax.axis_index("frame") >> 3

    def pairs(refs):
        first = pl.multiple_of(576 * y_lo, 64)
        second = pl.multiple_of(576 * (1 - y_lo), 64)
        places = (pl.ds(first, 576), pl.ds(second, 288), pl.ds(second + 288, 288))
        return [(ref, w_scr.at[rows]) for ref, rows in zip(refs, places)]

    for cond, refs in ((c == core, mine), (c != core, other)):

        @pl.when(cond)
        def _(refs=refs):
            launch(pairs(refs), sems)

    return [pltpu.make_async_copy(src, dst, sems.at[i]) for i, (src, dst) in enumerate(pairs(mine))]


def middle_kernel(o_in, clip_in, mod_ref, m0, m1, m2, n0, n1, n2, mid_out, out_ref, o_ref, clip_ref, mid_ref, w_scr, sems, w_sems):
    copies = launch([(o_in, o_ref), (clip_in, clip_ref)], sems)
    weights = fetch_projection(0, (m0, m1, m2), (n0, n1, n2), w_scr, w_sems)
    copies[0].wait()
    groups = [
        jnp.concatenate([o_ref[8 * (j >> 1) + 2 * g + (j & 1)] for j in range(4)], axis=0) for g in range(4)
    ]
    o = jnp.concatenate(groups, axis=1)
    for copy in weights:
        copy.wait()
    total = lax.dot_general(o, w_scr[...], NT, preferred_element_type=F32)
    copies[1].wait()
    mid = clip_ref[...].astype(F32) + mod_ref[2:3, :] * total
    mid_ref[...] = mid
    keep = pltpu.make_async_copy(mid_ref, mid_out, sems.at[2])
    keep.start()
    normed = normalize(mid, mod_ref[3:4, :], mod_ref[4:5, :])
    out = jnp.dot(spread(True), normed, preferred_element_type=F32).astype(BF)
    for f in range(16):
        out_ref[f] = out[32 * f : 32 * f + 24]
    keep.wait()


def temporal_kernel(x_ref, *refs):
    weights, (o_ref, y_scr, scr) = refs[:6], refs[6:]
    c = lax.axis_index("row") & 1
    y_lo = lax.axis_index("frame") >> 3
    x = jnp.dot(compact(True), unpack_chunks(x_ref, scr), preferred_element_type=F32).astype(BF)
    for t in range(2):
        y = [lax.dot_general(x, w[...], NT, preferred_element_type=F32) for w in weights[3 * t : 3 * t + 3]]
        y_scr[y_lo, c ^ t] = y[0]
        y_scr[1 - y_lo, c ^ t] = jnp.concatenate(y[1:], axis=1)

    def part(p):
        i, sub = p // 3, p % 3
        lo = 128 * (i % 8)
        if sub < 2:
            return y_scr[i // 8, sub, :, lo : lo + PAD]
        return jnp.concatenate([y_scr[i // 8, core, :, lo + 80 : lo + 120] for core in range(2)], axis=1)

    row = lax.broadcasted_iota(jnp.int32, (320, 320), 0)
    col = lax.broadcasted_iota(jnp.int32, (320, 320), 1)
    same = (row >> 6) == (col >> 6)
    heads = []
    for h in range(HEADS):
        q = (part(h) * SCALE).astype(BF)
        k = part(16 + h).astype(BF)
        v = part(32 + h).astype(BF)
        s = lax.dot_general(q, k, NT, preferred_element_type=F32)
        s = jnp.where(same, s, -1e30)
        m = jnp.max(s, axis=-1, keepdims=True)
        p = jnp.exp2(s - m)
        total = jnp.sum(p, axis=-1, keepdims=True)
        o = jnp.dot(p.astype(BF), v, preferred_element_type=F32) / total
        heads.append(o[:, :72].astype(BF))
    o = jnp.concatenate(heads, axis=1)
    out = jnp.dot(compact(False), o, preferred_element_type=F32).astype(BF)
    for f in range(16):
        o_ref[f] = out[32 * f : 32 * f + 24]


def final_kernel(o_in, mid_in, mod_ref, m0, m1, m2, n0, n1, n2, out_ref, o_ref, mid_ref, w_scr, scr, sems, w_sems):
    copies = launch([(mid_in, mid_ref), (o_in, o_ref)], sems)
    weights = fetch_projection(1, (m0, m1, m2), (n0, n1, n2), w_scr, w_sems)
    copies[1].wait()
    o = jnp.dot(spread(False), unpack_chunks(o_ref, scr), preferred_element_type=F32).astype(BF)
    for copy in weights:
        copy.wait()
    y = lax.dot_general(o, w_scr[...], NT, preferred_element_type=F32)
    copies[0].wait()
    out_ref[...] = (mid_ref[...] + mod_ref[5:6, :] * y).astype(BF)


def shift_x(value, d):
    pairs = [(r, (r & 9) | ((((r >> 1) + d) & 3) << 1)) for r in range(16)]
    return lax.ppermute(value, "row", pairs)


def swap_core(value):
    return lax.ppermute(value, "row", [(r, r ^ 1) for r in range(16)])


def swap_yh(value):
    return lax.ppermute(value, "row", [(r, r ^ 8) for r in range(16)])


def halves(value):
    half = value.shape[0] // 2
    return value[:half], value[half:]


def from_y_neighbours(parts):
    got = []
    for part, flip in zip(parts, (0, 8)):
        pairs = [(16 * f + r, 16 * (f ^ 8) + (r ^ flip)) for f in range(16) for r in range(16)]
        got.append(lax.ppermute(part, ("frame", "row"), pairs))
    return got


def gather_half(value):
    rings = [list(range(8)), list(range(8, 16))]
    return lax.all_gather(value, "frame", axis=0, tiled=True, axis_index_groups=rings)


def call(kernel, outs, n_in, scratch=(), mib=56, any_in=(), any_out=(), us=2):
    return pl.pallas_call(
        kernel,
        out_shape=outs,
        in_specs=[ANY if i in any_in else VMEM for i in range(n_in)],
        out_specs=[ANY if i in any_out else VMEM for i in range(len(outs))] if isinstance(outs, tuple) else ANY if any_out else VMEM,
        scratch_shapes=list(scratch),
        compiler_params=params(mib),
        cost_estimate=pl.CostEstimate(flops=us * 10**9, bytes_accessed=us * 10**6, transcendentals=0),
    )


def sds(shape, dtype=BF):
    return jax.ShapeDtypeStruct(shape, dtype)


def on_device(clip_tokens, modulation, w_sqkv, w_sout, w_tqkv, w_tout):
    frames_here, rows_here, patches, features = clip_tokens.shape
    tokens = rows_here * patches
    yh, x, c = place()

    proj, tq = call(prepare_kernel, (sds((72, D)), sds((128, D))), 3, mib=60)(w_tqkv.T, w_sout.T, w_tout.T)
    proj = gather_half(proj)
    tq = gather_half(tq)

    clip = clip_tokens.reshape(frames_here, tokens, features)
    keep, swap, give = call(norm_kernel, (sds((80, D)), sds((80, D)), sds((2, 80, D))), 2, mib=12)(clip, modulation)
    first = lax.dynamic_slice(w_sqkv, (576 * c, 0), (576, 216))
    keep, swap, give, first = lax.optimization_barrier((keep, swap, give, first))

    theirs = swap_yh(give)
    own = jnp.concatenate([keep, swap_core(swap)], axis=0)
    own, first = lax.optimization_barrier((own, first))
    first = lax.all_to_all(first.reshape(16, 36, 216), "frame", 0, 0, tiled=True)
    near = {d: shift_x(own, d) for d in (1, 3)}
    second = call(repack_kernel, sds((16, 40, 3 * GROUP)), 1, mib=12)(first)
    far = {}
    far[0] = jnp.concatenate([theirs[c], swap_core(theirs[1 - c])], axis=0)
    near[1], near[3], own, far[0], second = lax.optimization_barrier((near[1], near[3], own, far[0], second))
    near[0] = own
    near[2] = shift_x(own, 2)
    for d in (1, 2, 3):
        far[d] = shift_x(far[0], d)
    second = lax.all_to_all(second, "frame", 0, 0, tiled=True)
    _, proj = lax.optimization_barrier((near[2], proj))
    proj = [proj] + from_y_neighbours(halves(proj))
    near[2], far[1], far[2], far[3], second = lax.optimization_barrier((near[2], far[1], far[2], far[3], second))
    w_other = swap_core(second)

    o_s = call(
        spatial_kernel,
        sds((16, tokens, GROUP)),
        10,
        scratch=[
            pltpu.VMEM((1280, D), BF),
            pltpu.VMEM((2, 16, 40, 3 * GROUP), BF),
            pltpu.VMEM((D, 3 * GROUP), BF),
            pltpu.VMEM((4, 1280, 128), BF),
            pltpu.VMEM((4, 1280, 128), BF),
            pltpu.VMEM((4, 1280, 128), BF),
            pltpu.VMEM((4, 320, GROUP), BF),
            pltpu.SemaphoreType.DMA((10,)),
            pltpu.SemaphoreType.DMA((4, 4)),
        ],
        any_in=range(10),
        any_out=(0,),
        mib=52,
        us=15,
    )(*[half[d] for d in range(4) for half in (near, far)], second, w_other)
    o_s, *proj = lax.optimization_barrier((o_s, *proj))
    proj_other = [swap_core(v) for v in proj]
    o_s = lax.all_to_all(o_s, "row", 0, 0, tiled=True)
    _, tq, *parts = lax.optimization_barrier((o_s, tq, *halves(tq)))
    tq = [tq] + from_y_neighbours(parts)

    mid, chunks = call(
        middle_kernel,
        (sds((320, D), F32), sds((16, 24, D))),
        9,
        scratch=[
            pltpu.VMEM((16, tokens, GROUP), BF),
            pltpu.VMEM((320, D), BF),
            pltpu.VMEM((320, D), F32),
            pltpu.VMEM((D, D), BF),
            pltpu.SemaphoreType.DMA((3,)),
            pltpu.SemaphoreType.DMA((3,)),
        ],
        any_in=(0, 1, 3, 4, 5, 6, 7, 8),
        any_out=(0,),
        mib=60,
        us=4,
    )(o_s, clip.reshape(320, D), modulation, *proj, *proj_other)
    _, tq[0] = lax.optimization_barrier((chunks, tq[0]))
    tq_other = [swap_core(v) for v in tq]
    chunks = lax.all_to_all(chunks, "frame", 0, 0, tiled=True)

    o_t = call(
        temporal_kernel,
        sds((16, 24, D)),
        7,
        scratch=[pltpu.VMEM((2, 2, 320, 1024), F32), pltpu.VMEM((512, D), BF)],
        mib=40,
        us=12,
    )(chunks, *tq, *tq_other)
    o_t = lax.all_to_all(o_t, "frame", 0, 0, tiled=True)
    out = call(
        final_kernel,
        sds((320, D)),
        9,
        scratch=[
            pltpu.VMEM((16, 24, D), BF),
            pltpu.VMEM((320, D), F32),
            pltpu.VMEM((D, D), BF),
            pltpu.VMEM((512, D), BF),
            pltpu.SemaphoreType.DMA((2,)),
            pltpu.SemaphoreType.DMA((3,)),
        ],
        any_in=(0, 1, 3, 4, 5, 6, 7, 8),
        mib=60,
        us=4,
    )(o_t, mid, modulation, *proj, *proj_other)
    return out.reshape(frames_here, rows_here, patches, features)


def solution(mesh):
    in_specs = (
        P("frame", "row", None, None),
        P(),
        P(None, "frame"),
        P(None, "frame"),
        P(None, "frame"),
        P(None, "frame"),
    )
    out_specs = P("frame", "row", None, None)
    return jax.shard_map(
        on_device, mesh=mesh, in_specs=in_specs, out_specs=out_specs, check_vma=False
    )
```

```python
import functools
import math

import jax
import jax.numpy as jnp
from jax import lax
from jax.experimental import pallas as pl
from jax.experimental.pallas import tpu as pltpu
from jax.sharding import PartitionSpec as P

HEADS = 16
HEAD_DIM = 72
D = 1152
GROUP = 4 * HEAD_DIM
PAD = 80
BF = jnp.bfloat16
F32 = jnp.float32
SCALE = math.log2(math.e) / math.sqrt(HEAD_DIM)
VMEM = pl.BlockSpec(memory_space=pltpu.VMEM)
ANY = pl.BlockSpec(memory_space=pl.ANY)
NT = (((1,), (1,)), ((), ()))


def params(mib):
    return pltpu.CompilerParams(vmem_limit_bytes=mib * 1024 * 1024)


def normalize(inputs, shift, scale):
    average = jnp.mean(inputs, axis=-1, keepdims=True)
    centered = inputs - average
    variance = jnp.mean(centered * centered, axis=-1, keepdims=True)
    return (centered * lax.rsqrt(variance + 1e-06) * (1.0 + scale) + shift).astype(BF)


def place():
    r = lax.axis_index("row")
    return r >> 3, (r >> 1) & 3, r & 1


def norm_kernel(clip_ref, mod_ref, keep_ref, swap_ref, give_ref):
    yh, _, c = place()

    def normed(j):
        return normalize(clip_ref[j].astype(F32), mod_ref[0:1, :], mod_ref[1:2, :])

    keep_ref[...] = normed(2 * yh + c)
    swap_ref[...] = normed(2 * yh + 1 - c)
    for i in range(2):
        give_ref[i] = normed(2 * (1 - yh) + i)


def prepare_kernel(qkv_ref, sout_ref, tout_ref, proj_ref, out_ref):
    c = lax.axis_index("row") & 1
    for core, (lo, mid, width, proj) in enumerate(((0, 144, 40, sout_ref), (72, 184, 32, tout_ref))):

        @pl.when(c == core)
        def _(lo=lo, mid=mid, width=width, proj=proj):
            w = qkv_ref[...].astype(F32)
            rows = [w[lo : lo + 72], jnp.zeros((8, D), F32), w[mid : mid + width], jnp.zeros((48 - width, D), F32)]
            out_ref[...] = jnp.concatenate(rows, axis=0).astype(BF)
            proj_ref[...] = proj[...]


def repack_kernel(w_ref, out_ref):
    _, x, _ = place()
    for g in range(4):

        @pl.when(x == g)
        def _(g=g):
            cols = []
            for part in range(3):
                for h in range(4):
                    p = 16 * part + 4 * g + h
                    cols.append(w_ref[p // 3, :, 72 * (p % 3) : 72 * (p % 3) + 72])
            block = jnp.concatenate(cols, axis=1)
            block = jnp.concatenate([block, jnp.zeros((4, 3 * GROUP), BF)], axis=0)
            for f in range(16):
                out_ref[f] = block


def launch(pairs, sems):
    copies = [pltpu.make_async_copy(src, dst, sems.at[i]) for i, (src, dst) in enumerate(pairs)]
    for copy in copies:
        copy.start()
    return copies


def spatial_kernel(*refs):
    tokens, (w0, w1, o_ref, x_scr, w_in, w_scr, q_scr, k_scr, v_scr, out_scr, in_sems, out_sems) = refs[:8], refs[8:]
    yh, x, c = place()
    pairs = [(w, w_in.at[s]) for s, w in enumerate((w0, w1))]
    pairs += [(ref, x_scr.at[pl.ds(160 * i, 160)]) for i, ref in enumerate(tokens)]
    for s, copy in enumerate(launch(pairs, in_sems)[:2]):
        copy.wait()
        rows = pl.ds(pl.multiple_of(576 * (c ^ s), 64), 576)
        w_scr[rows, :] = jnp.concatenate([w_in[s, i, :36] for i in range(16)], axis=0)
    lane = lax.broadcasted_iota(jnp.int32, (320, 128 - HEAD_DIM), 1)
    zeros = jnp.zeros((320, 128 - HEAD_DIM), BF)
    ones = jnp.where(lane == 0, 1.0, 0.0).astype(BF)
    def project(i, carry):
        for near in range(2):
            half = x_scr.at[pl.ds(pl.multiple_of(320 * i + 160 * near, 32), 160)]
            pltpu.make_async_copy(tokens[0], half, in_sems.at[2 + 2 * i + near]).wait()
        rows = pl.ds(pl.multiple_of(320 * i, 64), 320)
        qkv = jnp.dot(x_scr[rows, :], w_scr[...], preferred_element_type=F32)
        for h in range(4):
            lo = 72 * h
            q = (qkv[:, lo : lo + 72] * SCALE).astype(BF)
            k = qkv[:, GROUP + lo : GROUP + lo + 72].astype(BF)
            v = qkv[:, 2 * GROUP + lo : 2 * GROUP + lo + 72].astype(BF)
            q_scr[h, rows, :] = jnp.concatenate([q, zeros], axis=1)
            k_scr[h, rows, :] = jnp.concatenate([k, zeros], axis=1)
            v_scr[h, rows, :] = jnp.concatenate([v, ones], axis=1)
        return carry

    lax.fori_loop(0, 4, project, 0)

    def outgoing(i, t):
        dest = (yh ^ (t >> 1)) * 8 + ((x - i) & 3) * 2 + (c ^ (t & 1))
        return pltpu.make_async_copy(out_scr.at[i, pl.ds(80 * t, 80)], o_ref.at[dest], out_sems.at[i, t])

    def step(i, carry):
        heads = []
        for h in range(4):
            q = q_scr[h, pl.ds(pl.multiple_of(320 * i, 64), 320), :]
            s = lax.dot_general(q, k_scr[h], NT, preferred_element_type=F32)
            m = jnp.max(s, axis=-1, keepdims=True)
            p = jnp.exp2(s - m).astype(BF)
            o = jnp.dot(p, v_scr[h], preferred_element_type=F32)
            heads.append((o[:, :72] / o[:, 72:73]).astype(BF))
        out_scr[i] = jnp.concatenate(heads, axis=1)
        for t in range(4):
            outgoing(i, t).start()
        return carry

    lax.fori_loop(0, 4, step, 0)
    for i in range(4):
        for t in range(4):
            outgoing(i, t).wait()


def spread(frame_major):
    if frame_major:
        row = lax.broadcasted_iota(jnp.int32, (512, 320), 0)
        col = lax.broadcasted_iota(jnp.int32, (512, 320), 1)
    else:
        row = lax.broadcasted_iota(jnp.int32, (320, 512), 1)
        col = lax.broadcasted_iota(jnp.int32, (320, 512), 0)
    f, t = row >> 5, row & 31
    j = (t * 13) >> 6
    want = 80 * j + 5 * f + (t - 5 * j)
    return jnp.where((t < 20) & (col == want), 1.0, 0.0).astype(BF)


def compact(narrow):
    if narrow:
        wide = lax.broadcasted_iota(jnp.int32, (320, 512), 1)
        thin = lax.broadcasted_iota(jnp.int32, (320, 512), 0)
    else:
        wide = lax.broadcasted_iota(jnp.int32, (512, 320), 0)
        thin = lax.broadcasted_iota(jnp.int32, (512, 320), 1)
    f, t = wide >> 5, wide & 31
    j = (t * 13) >> 6
    return jnp.where((t < 20) & (thin == 64 * (t - 5 * j) + 4 * f + j), 1.0, 0.0).astype(BF)


def unpack_chunks(ref, scr):
    zeros = jnp.zeros((8, D), BF)
    for f in range(16):
        scr[32 * f : 32 * f + 32, :] = jnp.concatenate([ref[f], zeros], axis=0)
    return scr[...]


def fetch_projection(core, mine, other, w_scr, sems):
    c = lax.axis_index("row") & 1
    y_lo = lax.axis_index("frame") >> 3

    def pairs(refs):
        first = pl.multiple_of(576 * y_lo, 64)
        second = pl.multiple_of(576 * (1 - y_lo), 64)
        places = (pl.ds(first, 576), pl.ds(second, 288), pl.ds(second + 288, 288))
        return [(ref, w_scr.at[rows]) for ref, rows in zip(refs, places)]

    for cond, refs in ((c == core, mine), (c != core, other)):

        @pl.when(cond)
        def _(refs=refs):
            launch(pairs(refs), sems)

    return [pltpu.make_async_copy(src, dst, sems.at[i]) for i, (src, dst) in enumerate(pairs(mine))]


def middle_kernel(o_in, clip_in, mod_ref, m0, m1, m2, n0, n1, n2, mid_out, out_ref, o_ref, clip_ref, mid_ref, w_scr, sems, w_sems):
    copies = launch([(o_in, o_ref), (clip_in, clip_ref)], sems)
    weights = fetch_projection(0, (m0, m1, m2), (n0, n1, n2), w_scr, w_sems)
    copies[0].wait()
    groups = [
        jnp.concatenate([o_ref[8 * (j >> 1) + 2 * g + (j & 1)] for j in range(4)], axis=0) for g in range(4)
    ]
    o = jnp.concatenate(groups, axis=1)
    for copy in weights:
        copy.wait()
    total = lax.dot_general(o, w_scr[...], NT, preferred_element_type=F32)
    copies[1].wait()
    mid = clip_ref[...].astype(F32) + mod_ref[2:3, :] * total
    mid_ref[...] = mid
    keep = pltpu.make_async_copy(mid_ref, mid_out, sems.at[2])
    keep.start()
    normed = normalize(mid, mod_ref[3:4, :], mod_ref[4:5, :])
    out = jnp.dot(spread(True), normed, preferred_element_type=F32).astype(BF)
    for f in range(16):
        out_ref[f] = out[32 * f : 32 * f + 24]
    keep.wait()


def temporal_kernel(x_ref, *refs):
    weights, (o_ref, y_scr, scr) = refs[:6], refs[6:]
    c = lax.axis_index("row") & 1
    y_lo = lax.axis_index("frame") >> 3
    x = jnp.dot(compact(True), unpack_chunks(x_ref, scr), preferred_element_type=F32).astype(BF)
    for t in range(2):
        y = [lax.dot_general(x, w[...], NT, preferred_element_type=F32) for w in weights[3 * t : 3 * t + 3]]
        y_scr[y_lo, c ^ t] = y[0]
        y_scr[1 - y_lo, c ^ t] = jnp.concatenate(y[1:], axis=1)

    def part(p):
        i, sub = p // 3, p % 3
        lo = 128 * (i % 8)
        if sub < 2:
            return y_scr[i // 8, sub, :, lo : lo + PAD]
        return jnp.concatenate([y_scr[i // 8, core, :, lo + 80 : lo + 120] for core in range(2)], axis=1)

    row = lax.broadcasted_iota(jnp.int32, (320, 320), 0)
    col = lax.broadcasted_iota(jnp.int32, (320, 320), 1)
    same = (row >> 6) == (col >> 6)
    heads = []
    for h in range(HEADS):
        q = (part(h) * SCALE).astype(BF)
        k = part(16 + h).astype(BF)
        v = part(32 + h).astype(BF)
        s = lax.dot_general(q, k, NT, preferred_element_type=F32)
        s = jnp.where(same, s, -1e30)
        m = jnp.max(s, axis=-1, keepdims=True)
        p = jnp.exp2(s - m)
        total = jnp.sum(p, axis=-1, keepdims=True)
        o = jnp.dot(p.astype(BF), v, preferred_element_type=F32) / total
        heads.append(o[:, :72].astype(BF))
    o = jnp.concatenate(heads, axis=1)
    out = jnp.dot(compact(False), o, preferred_element_type=F32).astype(BF)
    for f in range(16):
        o_ref[f] = out[32 * f : 32 * f + 24]


def final_kernel(o_in, mid_in, mod_ref, m0, m1, m2, n0, n1, n2, out_ref, o_ref, mid_ref, w_scr, scr, sems, w_sems):
    copies = launch([(mid_in, mid_ref), (o_in, o_ref)], sems)
    weights = fetch_projection(1, (m0, m1, m2), (n0, n1, n2), w_scr, w_sems)
    copies[1].wait()
    o = jnp.dot(spread(False), unpack_chunks(o_ref, scr), preferred_element_type=F32).astype(BF)
    for copy in weights:
        copy.wait()
    y = lax.dot_general(o, w_scr[...], NT, preferred_element_type=F32)
    copies[0].wait()
    out_ref[...] = (mid_ref[...] + mod_ref[5:6, :] * y).astype(BF)


def shift_x(value, d):
    pairs = [(r, (r & 9) | ((((r >> 1) + d) & 3) << 1)) for r in range(16)]
    return lax.ppermute(value, "row", pairs)


def swap_core(value):
    return lax.ppermute(value, "row", [(r, r ^ 1) for r in range(16)])


def swap_yh(value):
    return lax.ppermute(value, "row", [(r, r ^ 8) for r in range(16)])


def halves(value):
    half = value.shape[0] // 2
    return value[:half], value[half:]


def from_y_neighbours(parts):
    got = []
    for part, flip in zip(parts, (0, 8)):
        pairs = [(16 * f + r, 16 * (f ^ 8) + (r ^ flip)) for f in range(16) for r in range(16)]
        got.append(lax.ppermute(part, ("frame", "row"), pairs))
    return got


def gather_half(value):
    rings = [list(range(8)), list(range(8, 16))]
    return lax.all_gather(value, "frame", axis=0, tiled=True, axis_index_groups=rings)


def call(kernel, outs, n_in, scratch=(), mib=56, any_in=(), any_out=(), us=2):
    return pl.pallas_call(
        kernel,
        out_shape=outs,
        in_specs=[ANY if i in any_in else VMEM for i in range(n_in)],
        out_specs=[ANY if i in any_out else VMEM for i in range(len(outs))] if isinstance(outs, tuple) else ANY if any_out else VMEM,
        scratch_shapes=list(scratch),
        compiler_params=params(mib),
        cost_estimate=pl.CostEstimate(flops=us * 10**9, bytes_accessed=us * 10**6, transcendentals=0),
    )


def sds(shape, dtype=BF):
    return jax.ShapeDtypeStruct(shape, dtype)


def on_device(clip_tokens, modulation, w_sqkv, w_sout, w_tqkv, w_tout):
    frames_here, rows_here, patches, features = clip_tokens.shape
    tokens = rows_here * patches
    yh, x, c = place()

    proj, tq = call(prepare_kernel, (sds((72, D)), sds((128, D))), 3, mib=60)(w_tqkv.T, w_sout.T, w_tout.T)
    proj = gather_half(proj)
    tq = gather_half(tq)

    clip = clip_tokens.reshape(frames_here, tokens, features)
    keep, swap, give = call(norm_kernel, (sds((80, D)), sds((80, D)), sds((2, 80, D))), 2, mib=12)(clip, modulation)
    first = lax.dynamic_slice(w_sqkv, (576 * c, 0), (576, 216))
    keep, swap, give, first = lax.optimization_barrier((keep, swap, give, first))

    theirs = swap_yh(give)
    own = jnp.concatenate([keep, swap_core(swap)], axis=0)
    own, first = lax.optimization_barrier((own, first))
    first = lax.all_to_all(first.reshape(16, 36, 216), "frame", 0, 0, tiled=True)
    near = {d: shift_x(own, d) for d in (1, 3)}
    second = call(repack_kernel, sds((16, 40, 3 * GROUP)), 1, mib=12)(first)
    far = {}
    far[0] = jnp.concatenate([theirs[c], swap_core(theirs[1 - c])], axis=0)
    near[1], near[3], own, far[0], second = lax.optimization_barrier((near[1], near[3], own, far[0], second))
    near[0] = own
    near[2] = shift_x(own, 2)
    for d in (1, 2, 3):
        far[d] = shift_x(far[0], d)
    second = lax.all_to_all(second, "frame", 0, 0, tiled=True)
    _, proj = lax.optimization_barrier((near[2], proj))
    proj = [proj] + from_y_neighbours(halves(proj))
    near[2], far[1], far[2], far[3], second = lax.optimization_barrier((near[2], far[1], far[2], far[3], second))
    w_other = swap_core(second)

    o_s = call(
        spatial_kernel,
        sds((16, tokens, GROUP)),
        10,
        scratch=[
            pltpu.VMEM((1280, D), BF),
            pltpu.VMEM((2, 16, 40, 3 * GROUP), BF),
            pltpu.VMEM((D, 3 * GROUP), BF),
            pltpu.VMEM((4, 1280, 128), BF),
            pltpu.VMEM((4, 1280, 128), BF),
            pltpu.VMEM((4, 1280, 128), BF),
            pltpu.VMEM((4, 320, GROUP), BF),
            pltpu.SemaphoreType.DMA((10,)),
            pltpu.SemaphoreType.DMA((4, 4)),
        ],
        any_in=range(10),
        any_out=(0,),
        mib=52,
        us=15,
    )(*[half[d] for d in range(4) for half in (near, far)], second, w_other)
    o_s, *proj = lax.optimization_barrier((o_s, *proj))
    proj_other = [swap_core(v) for v in proj]
    o_s = lax.all_to_all(o_s, "row", 0, 0, tiled=True)
    _, tq, *parts = lax.optimization_barrier((o_s, tq, *halves(tq)))
    tq = [tq] + from_y_neighbours(parts)

    mid, chunks = call(
        middle_kernel,
        (sds((320, D), F32), sds((16, 24, D))),
        9,
        scratch=[
            pltpu.VMEM((16, tokens, GROUP), BF),
            pltpu.VMEM((320, D), BF),
            pltpu.VMEM((320, D), F32),
            pltpu.VMEM((D, D), BF),
            pltpu.SemaphoreType.DMA((3,)),
            pltpu.SemaphoreType.DMA((3,)),
        ],
        any_in=(0, 1, 3, 4, 5, 6, 7, 8),
        any_out=(0,),
        mib=60,
        us=4,
    )(o_s, clip.reshape(320, D), modulation, *proj, *proj_other)
    _, tq[0] = lax.optimization_barrier((chunks, tq[0]))
    tq_other = [swap_core(v) for v in tq]
    chunks = lax.all_to_all(chunks, "frame", 0, 0, tiled=True)

    o_t = call(
        temporal_kernel,
        sds((16, 24, D)),
        7,
        scratch=[pltpu.VMEM((2, 2, 320, 1024), F32), pltpu.VMEM((512, D), BF)],
        mib=40,
        us=12,
    )(chunks, *tq, *tq_other)
    o_t = lax.all_to_all(o_t, "frame", 0, 0, tiled=True)
    out = call(
        final_kernel,
        sds((320, D)),
        9,
        scratch=[
            pltpu.VMEM((16, 24, D), BF),
            pltpu.VMEM((320, D), F32),
            pltpu.VMEM((D, D), BF),
            pltpu.VMEM((512, D), BF),
            pltpu.SemaphoreType.DMA((2,)),
            pltpu.SemaphoreType.DMA((3,)),
        ],
        any_in=(0, 1, 3, 4, 5, 6, 7, 8),
        mib=60,
        us=4,
    )(o_t, mid, modulation, *proj, *proj_other)
    return out.reshape(frames_here, rows_here, patches, features)


def solution(mesh):
    in_specs = (
        P("frame", "row", None, None),
        P(),
        P(None, "frame"),
        P(None, "frame"),
        P(None, "frame"),
        P(None, "frame"),
    )
    out_specs = P("frame", "row", None, None)
    return jax.shard_map(
        on_device, mesh=mesh, in_specs=in_specs, out_specs=out_specs, check_vma=False
    )
```

```python
import functools
import math

import jax
import jax.numpy as jnp
from jax import lax
from jax.experimental import pallas as pl
from jax.experimental.pallas import tpu as pltpu
from jax.sharding import PartitionSpec as P

HEADS = 16
HEAD_DIM = 72
D = 1152
GROUP = 4 * HEAD_DIM
PAD = 80
BF = jnp.bfloat16
F32 = jnp.float32
SCALE = math.log2(math.e) / math.sqrt(HEAD_DIM)
VMEM = pl.BlockSpec(memory_space=pltpu.VMEM)
ANY = pl.BlockSpec(memory_space=pl.ANY)
NT = (((1,), (1,)), ((), ()))


def params(mib):
    return pltpu.CompilerParams(vmem_limit_bytes=mib * 1024 * 1024)


def normalize(inputs, shift, scale):
    average = jnp.mean(inputs, axis=-1, keepdims=True)
    centered = inputs - average
    variance = jnp.mean(centered * centered, axis=-1, keepdims=True)
    return (centered * lax.rsqrt(variance + 1e-06) * (1.0 + scale) + shift).astype(BF)


def place():
    r = lax.axis_index("row")
    return r >> 3, (r >> 1) & 3, r & 1


def norm_kernel(clip_ref, mod_ref, keep_ref, swap_ref, give_ref):
    yh, _, c = place()

    def normed(j):
        return normalize(clip_ref[j].astype(F32), mod_ref[0:1, :], mod_ref[1:2, :])

    keep_ref[...] = normed(2 * yh + c)
    swap_ref[...] = normed(2 * yh + 1 - c)
    for i in range(2):
        give_ref[i] = normed(2 * (1 - yh) + i)


def prepare_kernel(qkv_ref, sout_ref, tout_ref, proj_ref, out_ref):
    c = lax.axis_index("row") & 1
    for core, (lo, mid, width, proj) in enumerate(((0, 144, 40, sout_ref), (72, 184, 32, tout_ref))):

        @pl.when(c == core)
        def _(lo=lo, mid=mid, width=width, proj=proj):
            w = qkv_ref[...].astype(F32)
            rows = [w[lo : lo + 72], jnp.zeros((8, D), F32), w[mid : mid + width], jnp.zeros((48 - width, D), F32)]
            out_ref[...] = jnp.concatenate(rows, axis=0).astype(BF)
            proj_ref[...] = proj[...]


def repack_kernel(w_ref, out_ref):
    _, x, _ = place()
    for g in range(4):

        @pl.when(x == g)
        def _(g=g):
            cols = []
            for part in range(3):
                for h in range(4):
                    p = 16 * part + 4 * g + h
                    cols.append(w_ref[p // 3, :, 72 * (p % 3) : 72 * (p % 3) + 72])
            block = jnp.concatenate(cols, axis=1)
            block = jnp.concatenate([block, jnp.zeros((4, 3 * GROUP), BF)], axis=0)
            for f in range(16):
                out_ref[f] = block


def launch(pairs, sems):
    copies = [pltpu.make_async_copy(src, dst, sems.at[i]) for i, (src, dst) in enumerate(pairs)]
    for copy in copies:
        copy.start()
    return copies


def spatial_kernel(*refs):
    tokens, (w0, w1, o_ref, x_scr, w_in, w_scr, q_scr, k_scr, v_scr, out_scr, in_sems, out_sems) = refs[:8], refs[8:]
    yh, x, c = place()
    pairs = [(w, w_in.at[s]) for s, w in enumerate((w0, w1))]
    pairs += [(ref, x_scr.at[pl.ds(160 * i, 160)]) for i, ref in enumerate(tokens)]
    for s, copy in enumerate(launch(pairs, in_sems)[:2]):
        copy.wait()
        rows = pl.ds(pl.multiple_of(576 * (c ^ s), 64), 576)
        w_scr[rows, :] = jnp.concatenate([w_in[s, i, :36] for i in range(16)], axis=0)
    lane = lax.broadcasted_iota(jnp.int32, (320, 128 - HEAD_DIM), 1)
    zeros = jnp.zeros((320, 128 - HEAD_DIM), BF)
    ones = jnp.where(lane == 0, 1.0, 0.0).astype(BF)
    def project(i, carry):
        for near in range(2):
            half = x_scr.at[pl.ds(pl.multiple_of(320 * i + 160 * near, 32), 160)]
            pltpu.make_async_copy(tokens[0], half, in_sems.at[2 + 2 * i + near]).wait()
        rows = pl.ds(pl.multiple_of(320 * i, 64), 320)
        qkv = jnp.dot(x_scr[rows, :], w_scr[...], preferred_element_type=F32)
        for h in range(4):
            lo = 72 * h
            q = (qkv[:, lo : lo + 72] * SCALE).astype(BF)
            k = qkv[:, GROUP + lo : GROUP + lo + 72].astype(BF)
            v = qkv[:, 2 * GROUP + lo : 2 * GROUP + lo + 72].astype(BF)
            q_scr[h, rows, :] = jnp.concatenate([q, zeros], axis=1)
            k_scr[h, rows, :] = jnp.concatenate([k, zeros], axis=1)
            v_scr[h, rows, :] = jnp.concatenate([v, ones], axis=1)
        return carry

    lax.fori_loop(0, 4, project, 0)

    def outgoing(i, t):
        dest = (yh ^ (t >> 1)) * 8 + ((x - i) & 3) * 2 + (c ^ (t & 1))
        return pltpu.make_async_copy(out_scr.at[i, pl.ds(80 * t, 80)], o_ref.at[dest], out_sems.at[i, t])

    def step(i, carry):
        heads = []
        for h in range(4):
            q = q_scr[h, pl.ds(pl.multiple_of(320 * i, 64), 320), :]
            s = lax.dot_general(q, k_scr[h], NT, preferred_element_type=F32)
            m = jnp.max(s, axis=-1, keepdims=True)
            p = jnp.exp2(s - m).astype(BF)
            o = jnp.dot(p, v_scr[h], preferred_element_type=F32)
            heads.append((o[:, :72] / o[:, 72:73]).astype(BF))
        out_scr[i] = jnp.concatenate(heads, axis=1)
        for t in range(4):
            outgoing(i, t).start()
        return carry

    lax.fori_loop(0, 4, step, 0)
    for i in range(4):
        for t in range(4):
            outgoing(i, t).wait()


def spread(frame_major):
    if frame_major:
        row = lax.broadcasted_iota(jnp.int32, (512, 320), 0)
        col = lax.broadcasted_iota(jnp.int32, (512, 320), 1)
    else:
        row = lax.broadcasted_iota(jnp.int32, (320, 512), 1)
        col = lax.broadcasted_iota(jnp.int32, (320, 512), 0)
    f, t = row >> 5, row & 31
    j = (t * 13) >> 6
    want = 80 * j + 5 * f + (t - 5 * j)
    return jnp.where((t < 20) & (col == want), 1.0, 0.0).astype(BF)


def compact(narrow):
    if narrow:
        wide = lax.broadcasted_iota(jnp.int32, (320, 512), 1)
        thin = lax.broadcasted_iota(jnp.int32, (320, 512), 0)
    else:
        wide = lax.broadcasted_iota(jnp.int32, (512, 320), 0)
        thin = lax.broadcasted_iota(jnp.int32, (512, 320), 1)
    f, t = wide >> 5, wide & 31
    j = (t * 13) >> 6
    return jnp.where((t < 20) & (thin == 64 * (t - 5 * j) + 4 * f + j), 1.0, 0.0).astype(BF)


def unpack_chunks(ref, scr):
    zeros = jnp.zeros((8, D), BF)
    for f in range(16):
        scr[32 * f : 32 * f + 32, :] = jnp.concatenate([ref[f], zeros], axis=0)
    return scr[...]


def fetch_projection(core, mine, other, w_scr, sems):
    c = lax.axis_index("row") & 1
    y_lo = lax.axis_index("frame") >> 3

    def pairs(refs):
        first = pl.multiple_of(576 * y_lo, 64)
        second = pl.multiple_of(576 * (1 - y_lo), 64)
        places = (pl.ds(first, 576), pl.ds(second, 288), pl.ds(second + 288, 288))
        return [(ref, w_scr.at[rows]) for ref, rows in zip(refs, places)]

    for cond, refs in ((c == core, mine), (c != core, other)):

        @pl.when(cond)
        def _(refs=refs):
            launch(pairs(refs), sems)

    return [pltpu.make_async_copy(src, dst, sems.at[i]) for i, (src, dst) in enumerate(pairs(mine))]


def middle_kernel(o_in, clip_in, mod_ref, m0, m1, m2, n0, n1, n2, mid_out, out_ref, o_ref, clip_ref, mid_ref, w_scr, sems, w_sems):
    copies = launch([(o_in, o_ref), (clip_in, clip_ref)], sems)
    weights = fetch_projection(0, (m0, m1, m2), (n0, n1, n2), w_scr, w_sems)
    copies[0].wait()
    groups = [
        jnp.concatenate([o_ref[8 * (j >> 1) + 2 * g + (j & 1)] for j in range(4)], axis=0) for g in range(4)
    ]
    o = jnp.concatenate(groups, axis=1)
    for copy in weights:
        copy.wait()
    total = lax.dot_general(o, w_scr[...], NT, preferred_element_type=F32)
    copies[1].wait()
    mid = clip_ref[...].astype(F32) + mod_ref[2:3, :] * total
    mid_ref[...] = mid
    keep = pltpu.make_async_copy(mid_ref, mid_out, sems.at[2])
    keep.start()
    normed = normalize(mid, mod_ref[3:4, :], mod_ref[4:5, :])
    out = jnp.dot(spread(True), normed, preferred_element_type=F32).astype(BF)
    for f in range(16):
        out_ref[f] = out[32 * f : 32 * f + 24]
    keep.wait()


def temporal_kernel(x_ref, *refs):
    weights, (o_ref, y_scr, scr) = refs[:6], refs[6:]
    c = lax.axis_index("row") & 1
    y_lo = lax.axis_index("frame") >> 3
    x = jnp.dot(compact(True), unpack_chunks(x_ref, scr), preferred_element_type=F32).astype(BF)
    for t in range(2):
        y = [lax.dot_general(x, w[...], NT, preferred_element_type=F32) for w in weights[3 * t : 3 * t + 3]]
        y_scr[y_lo, c ^ t] = y[0]
        y_scr[1 - y_lo, c ^ t] = jnp.concatenate(y[1:], axis=1)

    def part(p):
        i, sub = p // 3, p % 3
        lo = 128 * (i % 8)
        if sub < 2:
            return y_scr[i // 8, sub, :, lo : lo + PAD]
        return jnp.concatenate([y_scr[i // 8, core, :, lo + 80 : lo + 120] for core in range(2)], axis=1)

    row = lax.broadcasted_iota(jnp.int32, (320, 320), 0)
    col = lax.broadcasted_iota(jnp.int32, (320, 320), 1)
    same = (row >> 6) == (col >> 6)
    heads = []
    for h in range(HEADS):
        q = (part(h) * SCALE).astype(BF)
        k = part(16 + h).astype(BF)
        v = part(32 + h).astype(BF)
        s = lax.dot_general(q, k, NT, preferred_element_type=F32)
        s = jnp.where(same, s, -1e30)
        m = jnp.max(s, axis=-1, keepdims=True)
        p = jnp.exp2(s - m)
        total = jnp.sum(p, axis=-1, keepdims=True)
        o = jnp.dot(p.astype(BF), v, preferred_element_type=F32) / total
        heads.append(o[:, :72].astype(BF))
    o = jnp.concatenate(heads, axis=1)
    out = jnp.dot(compact(False), o, preferred_element_type=F32).astype(BF)
    for f in range(16):
        o_ref[f] = out[32 * f : 32 * f + 24]


def final_kernel(o_in, mid_in, mod_ref, m0, m1, m2, n0, n1, n2, out_ref, o_ref, mid_ref, w_scr, scr, sems, w_sems):
    copies = launch([(mid_in, mid_ref), (o_in, o_ref)], sems)
    weights = fetch_projection(1, (m0, m1, m2), (n0, n1, n2), w_scr, w_sems)
    copies[1].wait()
    o = jnp.dot(spread(False), unpack_chunks(o_ref, scr), preferred_element_type=F32).astype(BF)
    for copy in weights:
        copy.wait()
    y = lax.dot_general(o, w_scr[...], NT, preferred_element_type=F32)
    copies[0].wait()
    out_ref[...] = (mid_ref[...] + mod_ref[5:6, :] * y).astype(BF)


def shift_x(value, d):
    pairs = [(r, (r & 9) | ((((r >> 1) + d) & 3) << 1)) for r in range(16)]
    return lax.ppermute(value, "row", pairs)


def swap_core(value):
    return lax.ppermute(value, "row", [(r, r ^ 1) for r in range(16)])


def swap_yh(value):
    return lax.ppermute(value, "row", [(r, r ^ 8) for r in range(16)])


def halves(value):
    half = value.shape[0] // 2
    return value[:half], value[half:]


def from_y_neighbours(parts):
    got = []
    for part, flip in zip(parts, (0, 8)):
        pairs = [(16 * f + r, 16 * (f ^ 8) + (r ^ flip)) for f in range(16) for r in range(16)]
        got.append(lax.ppermute(part, ("frame", "row"), pairs))
    return got


def gather_half(value):
    rings = [list(range(8)), list(range(8, 16))]
    return lax.all_gather(value, "frame", axis=0, tiled=True, axis_index_groups=rings)


def call(kernel, outs, n_in, scratch=(), mib=56, any_in=(), any_out=(), us=2):
    return pl.pallas_call(
        kernel,
        out_shape=outs,
        in_specs=[ANY if i in any_in else VMEM for i in range(n_in)],
        out_specs=[ANY if i in any_out else VMEM for i in range(len(outs))] if isinstance(outs, tuple) else ANY if any_out else VMEM,
        scratch_shapes=list(scratch),
        compiler_params=params(mib),
        cost_estimate=pl.CostEstimate(flops=us * 10**9, bytes_accessed=us * 10**6, transcendentals=0),
    )


def sds(shape, dtype=BF):
    return jax.ShapeDtypeStruct(shape, dtype)


def on_device(clip_tokens, modulation, w_sqkv, w_sout, w_tqkv, w_tout):
    frames_here, rows_here, patches, features = clip_tokens.shape
    tokens = rows_here * patches
    yh, x, c = place()

    proj, tq = call(prepare_kernel, (sds((72, D)), sds((128, D))), 3, mib=60)(w_tqkv.T, w_sout.T, w_tout.T)
    proj = gather_half(proj)
    tq = gather_half(tq)

    clip = clip_tokens.reshape(frames_here, tokens, features)
    keep, swap, give = call(norm_kernel, (sds((80, D)), sds((80, D)), sds((2, 80, D))), 2, mib=12)(clip, modulation)
    first = lax.dynamic_slice(w_sqkv, (576 * c, 0), (576, 216))
    keep, swap, give, first = lax.optimization_barrier((keep, swap, give, first))

    theirs = swap_yh(give)
    own = jnp.concatenate([keep, swap_core(swap)], axis=0)
    own, first = lax.optimization_barrier((own, first))
    first = lax.all_to_all(first.reshape(16, 36, 216), "frame", 0, 0, tiled=True)
    near = {d: shift_x(own, d) for d in (1, 3)}
    second = call(repack_kernel, sds((16, 40, 3 * GROUP)), 1, mib=12)(first)
    far = {}
    far[0] = jnp.concatenate([theirs[c], swap_core(theirs[1 - c])], axis=0)
    near[1], near[3], own, far[0], second = lax.optimization_barrier((near[1], near[3], own, far[0], second))
    near[0] = own
    near[2] = shift_x(own, 2)
    for d in (1, 2, 3):
        far[d] = shift_x(far[0], d)
    second = lax.all_to_all(second, "frame", 0, 0, tiled=True)
    _, proj = lax.optimization_barrier((near[2], proj))
    proj = [proj] + from_y_neighbours(halves(proj))
    near[2], far[1], far[2], far[3], second = lax.optimization_barrier((near[2], far[1], far[2], far[3], second))
    w_other = swap_core(second)

    o_s = call(
        spatial_kernel,
        sds((16, tokens, GROUP)),
        10,
        scratch=[
            pltpu.VMEM((1280, D), BF),
            pltpu.VMEM((2, 16, 40, 3 * GROUP), BF),
            pltpu.VMEM((D, 3 * GROUP), BF),
            pltpu.VMEM((4, 1280, 128), BF),
            pltpu.VMEM((4, 1280, 128), BF),
            pltpu.VMEM((4, 1280, 128), BF),
            pltpu.VMEM((4, 320, GROUP), BF),
            pltpu.SemaphoreType.DMA((10,)),
            pltpu.SemaphoreType.DMA((4, 4)),
        ],
        any_in=range(10),
        any_out=(0,),
        mib=52,
        us=15,
    )(*[half[d] for d in range(4) for half in (near, far)], second, w_other)
    o_s, *proj = lax.optimization_barrier((o_s, *proj))
    proj_other = [swap_core(v) for v in proj]
    o_s = lax.all_to_all(o_s, "row", 0, 0, tiled=True)
    near_out, tq, *parts = lax.optimization_barrier((proj_other[0], tq, *halves(tq)))
    proj_other[0] = near_out
    tq = [tq] + from_y_neighbours(parts)

    mid, chunks = call(
        middle_kernel,
        (sds((320, D), F32), sds((16, 24, D))),
        9,
        scratch=[
            pltpu.VMEM((16, tokens, GROUP), BF),
            pltpu.VMEM((320, D), BF),
            pltpu.VMEM((320, D), F32),
            pltpu.VMEM((D, D), BF),
            pltpu.SemaphoreType.DMA((3,)),
            pltpu.SemaphoreType.DMA((3,)),
        ],
        any_in=(0, 1, 3, 4, 5, 6, 7, 8),
        any_out=(0,),
        mib=60,
        us=4,
    )(o_s, clip.reshape(320, D), modulation, *proj, *proj_other)
    _, tq[0] = lax.optimization_barrier((chunks, tq[0]))
    tq_other = [swap_core(v) for v in tq]
    chunks = lax.all_to_all(chunks, "frame", 0, 0, tiled=True)

    o_t = call(
        temporal_kernel,
        sds((16, 24, D)),
        7,
        scratch=[pltpu.VMEM((2, 2, 320, 1024), F32), pltpu.VMEM((512, D), BF)],
        mib=40,
        us=12,
    )(chunks, *tq, *tq_other)
    o_t = lax.all_to_all(o_t, "frame", 0, 0, tiled=True)
    out = call(
        final_kernel,
        sds((320, D)),
        9,
        scratch=[
            pltpu.VMEM((16, 24, D), BF),
            pltpu.VMEM((320, D), F32),
            pltpu.VMEM((D, D), BF),
            pltpu.VMEM((512, D), BF),
            pltpu.SemaphoreType.DMA((2,)),
            pltpu.SemaphoreType.DMA((3,)),
        ],
        any_in=(0, 1, 3, 4, 5, 6, 7, 8),
        mib=60,
        us=4,
    )(o_t, mid, modulation, *proj, *proj_other)
    return out.reshape(frames_here, rows_here, patches, features)


def solution(mesh):
    in_specs = (
        P("frame", "row", None, None),
        P(),
        P(None, "frame"),
        P(None, "frame"),
        P(None, "frame"),
        P(None, "frame"),
    )
    out_specs = P("frame", "row", None, None)
    return jax.shard_map(
        on_device, mesh=mesh, in_specs=in_specs, out_specs=out_specs, check_vma=False
    )
```

```python
import functools
import math

import jax
import jax.numpy as jnp
from jax import lax
from jax.experimental import pallas as pl
from jax.experimental.pallas import tpu as pltpu
from jax.sharding import PartitionSpec as P

HEADS = 16
HEAD_DIM = 72
D = 1152
GROUP = 4 * HEAD_DIM
PAD = 80
BF = jnp.bfloat16
F32 = jnp.float32
SCALE = math.log2(math.e) / math.sqrt(HEAD_DIM)
VMEM = pl.BlockSpec(memory_space=pltpu.VMEM)
ANY = pl.BlockSpec(memory_space=pl.ANY)
NT = (((1,), (1,)), ((), ()))


def params(mib):
    return pltpu.CompilerParams(vmem_limit_bytes=mib * 1024 * 1024)


def normalize(inputs, shift, scale):
    average = jnp.mean(inputs, axis=-1, keepdims=True)
    centered = inputs - average
    variance = jnp.mean(centered * centered, axis=-1, keepdims=True)
    return (centered * lax.rsqrt(variance + 1e-06) * (1.0 + scale) + shift).astype(BF)


def place():
    r = lax.axis_index("row")
    return r >> 3, (r >> 1) & 3, r & 1


def norm_kernel(clip_ref, mod_ref, keep_ref, swap_ref, give_ref):
    yh, _, c = place()

    def normed(j):
        return normalize(clip_ref[j].astype(F32), mod_ref[0:1, :], mod_ref[1:2, :])

    keep_ref[...] = normed(2 * yh + c)
    swap_ref[...] = normed(2 * yh + 1 - c)
    for i in range(2):
        give_ref[i] = normed(2 * (1 - yh) + i)


def prepare_kernel(qkv_ref, sout_ref, tout_ref, proj_ref, out_ref):
    c = lax.axis_index("row") & 1
    for core, (lo, mid, width, proj) in enumerate(((0, 144, 40, sout_ref), (72, 184, 32, tout_ref))):

        @pl.when(c == core)
        def _(lo=lo, mid=mid, width=width, proj=proj):
            w = qkv_ref[...].astype(F32)
            rows = [w[lo : lo + 72], jnp.zeros((8, D), F32), w[mid : mid + width], jnp.zeros((48 - width, D), F32)]
            out_ref[...] = jnp.concatenate(rows, axis=0).astype(BF)
            proj_ref[...] = proj[...]


def repack_kernel(w_ref, out_ref):
    _, x, _ = place()
    for g in range(4):

        @pl.when(x == g)
        def _(g=g):
            cols = []
            for part in range(3):
                for h in range(4):
                    p = 16 * part + 4 * g + h
                    cols.append(w_ref[p // 3, :, 72 * (p % 3) : 72 * (p % 3) + 72])
            block = jnp.concatenate(cols, axis=1)
            block = jnp.concatenate([block, jnp.zeros((4, 3 * GROUP), BF)], axis=0)
            for f in range(16):
                out_ref[f] = block


def launch(pairs, sems):
    copies = [pltpu.make_async_copy(src, dst, sems.at[i]) for i, (src, dst) in enumerate(pairs)]
    for copy in copies:
        copy.start()
    return copies


def spatial_kernel(*refs):
    tokens, (w0, w1, o_ref, x_scr, w_in, w_scr, q_scr, k_scr, v_scr, out_scr, in_sems, out_sems) = refs[:8], refs[8:]
    yh, x, c = place()
    pairs = [(w, w_in.at[s]) for s, w in enumerate((w0, w1))]
    pairs += [(ref, x_scr.at[pl.ds(160 * i, 160)]) for i, ref in enumerate(tokens)]
    for s, copy in enumerate(launch(pairs, in_sems)[:2]):
        copy.wait()
        rows = pl.ds(pl.multiple_of(576 * (c ^ s), 64), 576)
        w_scr[rows, :] = jnp.concatenate([w_in[s, i, :36] for i in range(16)], axis=0)
    lane = lax.broadcasted_iota(jnp.int32, (320, 128 - HEAD_DIM), 1)
    zeros = jnp.zeros((320, 128 - HEAD_DIM), BF)
    ones = jnp.where(lane == 0, 1.0, 0.0).astype(BF)
    def project(i, carry):
        for near in range(2):
            half = x_scr.at[pl.ds(pl.multiple_of(320 * i + 160 * near, 32), 160)]
            pltpu.make_async_copy(tokens[0], half, in_sems.at[2 + 2 * i + near]).wait()
        rows = pl.ds(pl.multiple_of(320 * i, 64), 320)
        qkv = jnp.dot(x_scr[rows, :], w_scr[...], preferred_element_type=F32)
        for h in range(4):
            lo = 72 * h
            q = (qkv[:, lo : lo + 72] * SCALE).astype(BF)
            k = qkv[:, GROUP + lo : GROUP + lo + 72].astype(BF)
            v = qkv[:, 2 * GROUP + lo : 2 * GROUP + lo + 72].astype(BF)
            q_scr[h, rows, :] = jnp.concatenate([q, zeros], axis=1)
            k_scr[h, rows, :] = jnp.concatenate([k, zeros], axis=1)
            v_scr[h, rows, :] = jnp.concatenate([v, ones], axis=1)
        return carry

    lax.fori_loop(0, 4, project, 0)

    def outgoing(i, t):
        dest = (yh ^ (t >> 1)) * 8 + ((x - i) & 3) * 2 + (c ^ (t & 1))
        return pltpu.make_async_copy(out_scr.at[i, pl.ds(80 * t, 80)], o_ref.at[dest], out_sems.at[i, t])

    def step(i, carry):
        heads = []
        for h in range(4):
            q = q_scr[h, pl.ds(pl.multiple_of(320 * i, 64), 320), :]
            s = lax.dot_general(q, k_scr[h], NT, preferred_element_type=F32)
            m = jnp.max(s, axis=-1, keepdims=True)
            p = jnp.exp2(s - m).astype(BF)
            o = jnp.dot(p, v_scr[h], preferred_element_type=F32)
            heads.append((o[:, :72] / o[:, 72:73]).astype(BF))
        out_scr[i] = jnp.concatenate(heads, axis=1)
        for t in range(4):
            outgoing(i, t).start()
        return carry

    lax.fori_loop(0, 4, step, 0)
    for i in range(4):
        for t in range(4):
            outgoing(i, t).wait()


def spread(frame_major):
    if frame_major:
        row = lax.broadcasted_iota(jnp.int32, (512, 320), 0)
        col = lax.broadcasted_iota(jnp.int32, (512, 320), 1)
    else:
        row = lax.broadcasted_iota(jnp.int32, (320, 512), 1)
        col = lax.broadcasted_iota(jnp.int32, (320, 512), 0)
    f, t = row >> 5, row & 31
    j = (t * 13) >> 6
    want = 80 * j + 5 * f + (t - 5 * j)
    return jnp.where((t < 20) & (col == want), 1.0, 0.0).astype(BF)


def compact(narrow):
    if narrow:
        wide = lax.broadcasted_iota(jnp.int32, (320, 512), 1)
        thin = lax.broadcasted_iota(jnp.int32, (320, 512), 0)
    else:
        wide = lax.broadcasted_iota(jnp.int32, (512, 320), 0)
        thin = lax.broadcasted_iota(jnp.int32, (512, 320), 1)
    f, t = wide >> 5, wide & 31
    j = (t * 13) >> 6
    return jnp.where((t < 20) & (thin == 64 * (t - 5 * j) + 4 * f + j), 1.0, 0.0).astype(BF)


def unpack_chunks(ref, scr):
    zeros = jnp.zeros((8, D), BF)
    for f in range(16):
        scr[32 * f : 32 * f + 32, :] = jnp.concatenate([ref[f], zeros], axis=0)
    return scr[...]


def fetch_projection(core, mine, other, w_scr, sems):
    c = lax.axis_index("row") & 1
    y_lo = lax.axis_index("frame") >> 3

    def pairs(refs):
        first = pl.multiple_of(576 * y_lo, 64)
        second = pl.multiple_of(576 * (1 - y_lo), 64)
        places = (pl.ds(first, 576), pl.ds(second, 288), pl.ds(second + 288, 288))
        return [(ref, w_scr.at[rows]) for ref, rows in zip(refs, places)]

    for cond, refs in ((c == core, mine), (c != core, other)):

        @pl.when(cond)
        def _(refs=refs):
            launch(pairs(refs), sems)

    return [pltpu.make_async_copy(src, dst, sems.at[i]) for i, (src, dst) in enumerate(pairs(mine))]


def middle_kernel(o_in, clip_in, mod_ref, m0, m1, m2, n0, n1, n2, mid_out, out_ref, o_ref, clip_ref, mid_ref, w_scr, sems, w_sems):
    copies = launch([(o_in, o_ref), (clip_in, clip_ref)], sems)
    weights = fetch_projection(0, (m0, m1, m2), (n0, n1, n2), w_scr, w_sems)
    copies[0].wait()
    groups = [
        jnp.concatenate([o_ref[8 * (j >> 1) + 2 * g + (j & 1)] for j in range(4)], axis=0) for g in range(4)
    ]
    o = jnp.concatenate(groups, axis=1)
    for copy in weights:
        copy.wait()
    total = lax.dot_general(o, w_scr[...], NT, preferred_element_type=F32)
    copies[1].wait()
    mid = clip_ref[...].astype(F32) + mod_ref[2:3, :] * total
    mid_ref[...] = mid
    keep = pltpu.make_async_copy(mid_ref, mid_out, sems.at[2])
    keep.start()
    normed = normalize(mid, mod_ref[3:4, :], mod_ref[4:5, :])
    out = jnp.dot(spread(True), normed, preferred_element_type=F32).astype(BF)
    for f in range(16):
        out_ref[f] = out[32 * f : 32 * f + 24]
    keep.wait()


def temporal_kernel(x_ref, *refs):
    weights, (o_ref, y_scr, scr) = refs[:6], refs[6:]
    c = lax.axis_index("row") & 1
    y_lo = lax.axis_index("frame") >> 3
    x = jnp.dot(compact(True), unpack_chunks(x_ref, scr), preferred_element_type=F32).astype(BF)
    for t in range(2):
        y = [lax.dot_general(x, w[...], NT, preferred_element_type=F32) for w in weights[3 * t : 3 * t + 3]]
        y_scr[y_lo, c ^ t] = y[0]
        y_scr[1 - y_lo, c ^ t] = jnp.concatenate(y[1:], axis=1)

    def part(p):
        i, sub = p // 3, p % 3
        lo = 128 * (i % 8)
        if sub < 2:
            return y_scr[i // 8, sub, :, lo : lo + PAD]
        return jnp.concatenate([y_scr[i // 8, core, :, lo + 80 : lo + 120] for core in range(2)], axis=1)

    row = lax.broadcasted_iota(jnp.int32, (320, 320), 0)
    col = lax.broadcasted_iota(jnp.int32, (320, 320), 1)
    same = (row >> 6) == (col >> 6)
    heads = []
    for h in range(HEADS):
        q = (part(h) * SCALE).astype(BF)
        k = part(16 + h).astype(BF)
        v = part(32 + h).astype(BF)
        s = lax.dot_general(q, k, NT, preferred_element_type=F32)
        s = jnp.where(same, s, -1e30)
        m = jnp.max(s, axis=-1, keepdims=True)
        p = jnp.exp2(s - m)
        total = jnp.sum(p, axis=-1, keepdims=True)
        o = jnp.dot(p.astype(BF), v, preferred_element_type=F32) / total
        heads.append(o[:, :72].astype(BF))
    o = jnp.concatenate(heads, axis=1)
    out = jnp.dot(compact(False), o, preferred_element_type=F32).astype(BF)
    for f in range(16):
        o_ref[f] = out[32 * f : 32 * f + 24]


def final_kernel(o_in, mid_in, mod_ref, m0, m1, m2, n0, n1, n2, out_ref, o_ref, mid_ref, w_scr, scr, sems, w_sems):
    copies = launch([(mid_in, mid_ref), (o_in, o_ref)], sems)
    weights = fetch_projection(1, (m0, m1, m2), (n0, n1, n2), w_scr, w_sems)
    copies[1].wait()
    o = jnp.dot(spread(False), unpack_chunks(o_ref, scr), preferred_element_type=F32).astype(BF)
    for copy in weights:
        copy.wait()
    y = lax.dot_general(o, w_scr[...], NT, preferred_element_type=F32)
    copies[0].wait()
    out_ref[...] = (mid_ref[...] + mod_ref[5:6, :] * y).astype(BF)


def shift_x(value, d):
    pairs = [(r, (r & 9) | ((((r >> 1) + d) & 3) << 1)) for r in range(16)]
    return lax.ppermute(value, "row", pairs)


def swap_core(value):
    return lax.ppermute(value, "row", [(r, r ^ 1) for r in range(16)])


def swap_yh(value):
    return lax.ppermute(value, "row", [(r, r ^ 8) for r in range(16)])


def halves(value):
    half = value.shape[0] // 2
    return value[:half], value[half:]


def from_y_neighbours(parts):
    got = []
    for part, flip in zip(parts, (0, 8)):
        pairs = [(16 * f + r, 16 * (f ^ 8) + (r ^ flip)) for f in range(16) for r in range(16)]
        got.append(lax.ppermute(part, ("frame", "row"), pairs))
    return got


def gather_half(value):
    rings = [list(range(8)), list(range(8, 16))]
    return lax.all_gather(value, "frame", axis=0, tiled=True, axis_index_groups=rings)


def call(kernel, outs, n_in, scratch=(), mib=56, any_in=(), any_out=(), us=2):
    return pl.pallas_call(
        kernel,
        out_shape=outs,
        in_specs=[ANY if i in any_in else VMEM for i in range(n_in)],
        out_specs=[ANY if i in any_out else VMEM for i in range(len(outs))] if isinstance(outs, tuple) else ANY if any_out else VMEM,
        scratch_shapes=list(scratch),
        compiler_params=params(mib),
        cost_estimate=pl.CostEstimate(flops=us * 10**9, bytes_accessed=us * 10**6, transcendentals=0),
    )


def sds(shape, dtype=BF):
    return jax.ShapeDtypeStruct(shape, dtype)


def on_device(clip_tokens, modulation, w_sqkv, w_sout, w_tqkv, w_tout):
    frames_here, rows_here, patches, features = clip_tokens.shape
    tokens = rows_here * patches
    yh, x, c = place()

    proj, tq = call(prepare_kernel, (sds((72, D)), sds((128, D))), 3, mib=60)(w_tqkv.T, w_sout.T, w_tout.T)
    proj = gather_half(proj)
    tq = gather_half(tq)

    clip = clip_tokens.reshape(frames_here, tokens, features)
    keep, swap, give = call(norm_kernel, (sds((80, D)), sds((80, D)), sds((2, 80, D))), 2, mib=12)(clip, modulation)
    first = lax.dynamic_slice(w_sqkv, (576 * c, 0), (576, 216))
    keep, swap, give, first = lax.optimization_barrier((keep, swap, give, first))

    theirs = swap_yh(give)
    own = jnp.concatenate([keep, swap_core(swap)], axis=0)
    own, first = lax.optimization_barrier((own, first))
    first = lax.all_to_all(first.reshape(16, 36, 216), "frame", 0, 0, tiled=True)
    near = {d: shift_x(own, d) for d in (1, 3)}
    second = call(repack_kernel, sds((16, 40, 3 * GROUP)), 1, mib=12)(first)
    far = {}
    far[0] = jnp.concatenate([theirs[c], swap_core(theirs[1 - c])], axis=0)
    near[1], near[3], own, far[0], second = lax.optimization_barrier((near[1], near[3], own, far[0], second))
    near[0] = own
    near[2] = shift_x(own, 2)
    for d in (1, 2, 3):
        far[d] = shift_x(far[0], d)
    second = lax.all_to_all(second, "frame", 0, 0, tiled=True)
    _, proj = lax.optimization_barrier((near[2], proj))
    proj = [proj] + from_y_neighbours(halves(proj))
    near[2], far[1], far[2], far[3], second = lax.optimization_barrier((near[2], far[1], far[2], far[3], second))
    w_other = swap_core(second)

    o_s = call(
        spatial_kernel,
        sds((16, tokens, GROUP)),
        10,
        scratch=[
            pltpu.VMEM((1280, D), BF),
            pltpu.VMEM((2, 16, 40, 3 * GROUP), BF),
            pltpu.VMEM((D, 3 * GROUP), BF),
            pltpu.VMEM((4, 1280, 128), BF),
            pltpu.VMEM((4, 1280, 128), BF),
            pltpu.VMEM((4, 1280, 128), BF),
            pltpu.VMEM((4, 320, GROUP), BF),
            pltpu.SemaphoreType.DMA((10,)),
            pltpu.SemaphoreType.DMA((4, 4)),
        ],
        any_in=range(10),
        any_out=(0,),
        mib=52,
        us=15,
    )(*[half[d] for d in range(4) for half in (near, far)], second, w_other)
    o_s, *proj = lax.optimization_barrier((o_s, *proj))
    proj_other = [swap_core(v) for v in proj]
    o_s = lax.all_to_all(o_s, "row", 0, 0, tiled=True)
    near_out, tq, *parts = lax.optimization_barrier((proj_other[0], tq, *halves(tq)))
    proj_other[0] = near_out
    tq = [tq] + from_y_neighbours(parts)

    mid, chunks = call(
        middle_kernel,
        (sds((320, D), F32), sds((16, 24, D))),
        9,
        scratch=[
            pltpu.VMEM((16, tokens, GROUP), BF),
            pltpu.VMEM((320, D), BF),
            pltpu.VMEM((320, D), F32),
            pltpu.VMEM((D, D), BF),
            pltpu.SemaphoreType.DMA((3,)),
            pltpu.SemaphoreType.DMA((3,)),
        ],
        any_in=(0, 1, 3, 4, 5, 6, 7, 8),
        any_out=(0,),
        mib=48,
        us=4,
    )(o_s, clip.reshape(320, D), modulation, *proj, *proj_other)
    _, tq[0] = lax.optimization_barrier((chunks, tq[0]))
    tq_other = [swap_core(v) for v in tq]
    chunks = lax.all_to_all(chunks, "frame", 0, 0, tiled=True)

    o_t = call(
        temporal_kernel,
        sds((16, 24, D)),
        7,
        scratch=[pltpu.VMEM((2, 2, 320, 1024), F32), pltpu.VMEM((512, D), BF)],
        mib=40,
        us=12,
    )(chunks, *tq, *tq_other)
    o_t = lax.all_to_all(o_t, "frame", 0, 0, tiled=True)
    out = call(
        final_kernel,
        sds((320, D)),
        9,
        scratch=[
            pltpu.VMEM((16, 24, D), BF),
            pltpu.VMEM((320, D), F32),
            pltpu.VMEM((D, D), BF),
            pltpu.VMEM((512, D), BF),
            pltpu.SemaphoreType.DMA((2,)),
            pltpu.SemaphoreType.DMA((3,)),
        ],
        any_in=(0, 1, 3, 4, 5, 6, 7, 8),
        mib=60,
        us=4,
    )(o_t, mid, modulation, *proj, *proj_other)
    return out.reshape(frames_here, rows_here, patches, features)


def solution(mesh):
    in_specs = (
        P("frame", "row", None, None),
        P(),
        P(None, "frame"),
        P(None, "frame"),
        P(None, "frame"),
        P(None, "frame"),
    )
    out_specs = P("frame", "row", None, None)
    return jax.shard_map(
        on_device, mesh=mesh, in_specs=in_specs, out_specs=out_specs, check_vma=False
    )
```
